1024 devices in a mesh: shard: 64 (over y, z), replica: 16 (over x, core).
Axes of the slice: x: 8, y: 8, z: 8, core: 2. Of those that a mesh axis runs over, the one named last changes fastest.
Arguments:
- grads: bfloat16 [16, 4096, 64, 256], P('replica', 'shard'), may hold values from -0.59765625 to 0.59765625
- slots: int32 [16, 64, 8, 4096], P('replica', 'shard'), may hold values from 0 to 1023
- lengths: int32 [16, 64, 4096], P('replica', 'shard'), may hold values from 1 to 8
- rows: float32 [65536, 256], P(('shard', 'replica')), may hold values from -6 to 6
- accum: float32 [65536], P(('shard', 'replica')), may hold values from 0.1 to 10
Outputs:
- new_rows: float32 [65536, 256], P(('shard', 'replica'))
- new_accum: float32 [65536], P(('shard', 'replica'))
- serving: bfloat16 [65536, 256], P('shard')
The draws below stay inside these ranges and needn't reach their ends.
All inputs are finite; a program needn't handle non-finite values.
Results may differ from the reference program's by a relative error of at most 0.012.
Values may be sent and summed in bfloat16 or wider, within the bound.
No kernel may reach another device: no remote copies, remote signals or barrier semaphores. Data moves between devices by JAX's collectives and lax.ppermute only.
A program may use at most 32 MiB of HBM per device.

```python
import math
import jax
import jax.numpy as jnp
import numpy as np
from jax import lax

W = 256
L = 8
SLAB = 1024
F = 64
GS = 4096
N_REPLICA = 16


def set_ends(values, key, least, top_value):
    index_at = [jax.random.randint(jax.random.fold_in(key, axis), (), 0, length) for axis, length in enumerate(values.shape)]
    longest = values.shape.index(max(values.shape))
    neighbour = index_at[:longest] + [(index_at[longest] + 1) % values.shape[longest]] + index_at[longest + 1:]
    return values.at[tuple(index_at)].set(least).at[tuple(neighbour)].set(top_value)


def shard_levels(stream_key, extent, cuts, smallest, top_value):
    def one(axis_at, shards_of):
        draws = jax.random.uniform(jax.random.fold_in(jax.random.fold_in(stream_key, 6), axis_at), (shards_of,), jnp.float32, smallest / len(cuts), top_value / len(cuts))
        return jnp.repeat(jnp.exp(draws), extent[axis_at] // shards_of).reshape((-1,) + (1,) * (len(extent) - axis_at - 1))

    level = one(*cuts[0])
    for cut in cuts[1:]:
        level = level * one(*cut)
    return level


def cumulative_ranks(number_of, slope):
    loads = [(1 << 20) // math.isqrt(standing ** slope) + 1 for standing in range(1, number_of + 1)]
    width = 1 + sum(loads) // (1 << 30)
    return np.cumsum(np.array([max(1, weight // width) for weight in loads]))


def skewed_ids(key, extent, number_of, skew):
    listing = cumulative_ranks(number_of, skew)
    lot = jax.random.randint(jax.random.fold_in(key, 1), extent, 0, int(listing[number_of - 1]))
    standing = jnp.searchsorted(jnp.asarray(listing, jnp.int32), lot, side="right")
    return jax.random.permutation(jax.random.fold_in(key, 2), number_of)[standing].astype(jnp.int32)


def normal_values(key, shape, width, limit, cuts=(), kind=jnp.bfloat16):
    loudness = shard_levels(key, shape, cuts, -0.22, 0.18) if cuts else 1.0
    values = jax.random.normal(key, shape, jnp.float32) * width * loudness
    return jnp.minimum(jnp.maximum(values, -limit), limit).astype(kind)


def setup_inputs(seed: int = 0) -> dict:
    arg_keys = jax.random.split(jax.random.key(seed), 6)
    grads = normal_values(arg_keys[0], (N_REPLICA, GS, F, W), 0.1, 0.59765625, ((0, 16), (1, 64)))
    slots = set_ends(skewed_ids(arg_keys[1], (N_REPLICA, F, L, GS), SLAB, 1), jax.random.fold_in(arg_keys[1], 3), 0, SLAB - 1).astype(jnp.int32)
    lengths = set_ends(jax.random.randint(arg_keys[2], (N_REPLICA, F, GS), 1, L + 1), jax.random.fold_in(arg_keys[2], 1), 1, L).astype(jnp.int32)
    rows = normal_values(arg_keys[3], (F * SLAB, W), 1.0, 6.0, ((0, 1024),), jnp.float32)
    accum = jnp.clip(jnp.exp(math.log(10.0) - 4.6051702 * jax.random.uniform(arg_keys[4], (F * SLAB,), jnp.float32) ** shard_levels(arg_keys[4], (F * SLAB,), ((0, 1024),), -0.2, 0.2)), 0.1, 10.0)
    return dict(grads=grads, slots=slots, lengths=lengths, rows=rows, accum=accum)


step_rate = 0.5
epsilon = 1e-08

def reference(grads, slots, lengths, rows, accum):
    positions = jnp.arange(L, dtype=jnp.int32)

    def per_table(table):
        pooled = grads[:, :, table, :].astype(jnp.float32)
        table_slots = slots[:, table]
        table_lens = lengths[:, table]
        live_ids = (positions[None, :, None] < table_lens[:, None, :]).astype(jnp.float32)
        weighted = pooled[:, None, :, :] * live_ids[..., None]
        return jax.ops.segment_sum(weighted.reshape(-1, W), table_slots.reshape(-1), num_segments=SLAB)
    row_grad = lax.map(per_table, jnp.arange(F, dtype=jnp.int32)).reshape(F * SLAB, W)
    new_accum = accum + lax.optimization_barrier(jnp.mean(row_grad * row_grad, axis=1))
    new_rows = rows - step_rate * row_grad / (jnp.sqrt(new_accum)[:, None] + epsilon)
    return (new_rows, new_accum, new_rows.astype(jnp.bfloat16))
```

```python
import jax
import jax.numpy as jnp
from jax import lax
from jax.experimental import pallas as pl
from jax.experimental.pallas import tpu as pltpu
from jax.sharding import PartitionSpec as P

SLAB = 1024
STEP_RATE = 0.5
EPSILON = 1e-08


def count_kernel(slots_ref, lens_ref, counts_ref):
    positions, width = slots_ref.shape
    slab = counts_ref.shape[0]
    tall = 64
    place = lax.broadcasted_iota(jnp.int32, (positions, width), 0)
    live = jnp.where(place < lens_ref[...], slots_ref[...], -1)
    ids = [
        jnp.broadcast_to(live[p : p + 1, :], (tall, width)).astype(jnp.int16)
        for p in range(positions)
    ]
    row = lax.broadcasted_iota(jnp.int32, (tall, width), 0).astype(jnp.int16)
    one = jnp.ones((tall, width), jnp.bfloat16)
    zero = jnp.zeros((tall, width), jnp.bfloat16)

    def rows_block(i, carry):
        first = i * tall
        mine = row + first.astype(jnp.int16)
        total = zero
        for p in range(positions):
            total = total + jnp.where(ids[p] == mine, one, zero)
        counts_ref[pl.ds(pl.multiple_of(first, tall), tall), :] = total
        return carry

    lax.fori_loop(0, slab // tall, rows_block, 0)


def count_matrix(slots, lens):
    positions, samples = slots.shape
    width = 256
    return pl.pallas_call(
        count_kernel,
        grid=(samples // width,),
        in_specs=[
            pl.BlockSpec((positions, width), lambda i: (0, i)),
            pl.BlockSpec((1, width), lambda i: (0, i)),
        ],
        out_specs=pl.BlockSpec((SLAB, width), lambda i: (0, i)),
        out_shape=jax.ShapeDtypeStruct((SLAB, samples), jnp.bfloat16),
        compiler_params=pltpu.CompilerParams(vmem_limit_bytes=16 * 1024 * 1024),
        cost_estimate=pl.CostEstimate(
            flops=16 * SLAB * samples, bytes_accessed=2 * SLAB * samples, transcendentals=0
        ),
        name="counts",
    )(slots, lens)


def shards(grads, slots, lengths, rows, accum):
    arrived = lax.all_to_all(grads, "shard", split_axis=2, concat_axis=1, tiled=True)
    samples, width = arrived.shape[1], arrived.shape[3]
    counts = count_matrix(slots.reshape(slots.shape[2], samples), lengths.reshape(1, samples))
    partial = jnp.dot(
        counts, arrived.reshape(samples, width), preferred_element_type=jnp.float32
    ).astype(jnp.bfloat16)
    share = rows.shape[0]
    parts = lax.all_to_all(
        partial.reshape(SLAB // share, share, width), "replica", 0, 0, tiled=True
    )
    row_grad = jnp.sum(parts.astype(jnp.float32), axis=0)
    new_accum = accum + jnp.mean(row_grad * row_grad, axis=1)
    new_rows = rows - STEP_RATE * row_grad / (jnp.sqrt(new_accum)[:, None] + EPSILON)
    serving = lax.all_gather(new_rows.astype(jnp.bfloat16), "replica", axis=0, tiled=True)
    return new_rows, new_accum, serving


def solution(mesh):
    return jax.shard_map(
        shards,
        mesh=mesh,
        in_specs=(
            P("replica", "shard", None, None),
            P("replica", "shard", None, None),
            P("replica", "shard", None),
            P(("shard", "replica"), None),
            P(("shard", "replica")),
        ),
        out_specs=(P(("shard", "replica"), None), P(("shard", "replica")), P("shard", None)),
        check_vma=False,
    )
```

```python
import jax
import jax.numpy as jnp
from jax import lax
from jax.experimental import pallas as pl
from jax.experimental.pallas import tpu as pltpu
from jax.sharding import Mesh, PartitionSpec as P

SLAB = 1024
STEP_RATE = 0.5
EPSILON = 1e-08
CORES = 2
VMEM = 56 * 1024 * 1024


def spread_kernel(grads_ref, out_ref):
    side = grads_ref.shape[0]
    features, width = grads_ref.shape[1:]
    half = width // CORES
    out_at = lax.broadcasted_iota(jnp.int32, (side * side, side * side), 0)
    in_at = lax.broadcasted_iota(jnp.int32, (side * side, side * side), 1)
    moved = (out_at % side) * side + out_at // side
    permutation = jnp.where(in_at == moved, 1.0, 0.0).astype(jnp.bfloat16)
    for first in range(0, features, side):
        block = grads_ref[:, first : first + side, :].reshape(side * side, width)
        turned = jnp.dot(permutation, block, preferred_element_type=jnp.float32)
        turned = turned.astype(jnp.bfloat16).reshape(side, side, width)
        for core in range(CORES):
            out_ref[first : first + side, core] = turned[:, :, core * half : (core + 1) * half]


def spread(grads):
    samples, features, width = grads.shape
    side = 16
    return pl.pallas_call(
        spread_kernel,
        grid=(samples // side,),
        in_specs=[pl.BlockSpec((side, features, width), lambda i: (i, 0, 0))],
        out_specs=pl.BlockSpec((features, CORES, side, width // CORES), lambda i: (0, 0, i, 0)),
        out_shape=jax.ShapeDtypeStruct((features, CORES, samples, width // CORES), grads.dtype),
        compiler_params=pltpu.CompilerParams(vmem_limit_bytes=VMEM),
        name="spread",
    )(grads)


def count_kernel(ids_ref, counts_ref):
    positions, width = ids_ref.shape[1:]
    slab = counts_ref.shape[1]
    tall = 64
    ids = [
        jnp.broadcast_to(ids_ref[0, p : p + 1, :], (tall, width)).astype(jnp.int16)
        for p in range(positions)
    ]
    row = lax.broadcasted_iota(jnp.int32, (tall, width), 0).astype(jnp.int16)
    one = jnp.ones((tall, width), jnp.bfloat16)
    zero = jnp.zeros((tall, width), jnp.bfloat16)

    def rows_block(i, carry):
        first = i * tall
        mine = row + first.astype(jnp.int16)
        total = zero
        for p in range(positions):
            total = total + jnp.where(ids[p] == mine, one, zero)
        counts_ref[0, pl.ds(pl.multiple_of(first, tall), tall), :] = total
        return carry

    lax.fori_loop(0, slab // tall, rows_block, 0)


def count_matrix(ids):
    cores, positions, samples = ids.shape
    width = 256
    return pl.pallas_call(
        count_kernel,
        grid=(cores, samples // width),
        in_specs=[pl.BlockSpec((1, positions, width), lambda c, i: (c, 0, i))],
        out_specs=pl.BlockSpec((1, SLAB, width), lambda c, i: (c, 0, i)),
        out_shape=jax.ShapeDtypeStruct((cores, SLAB, samples), jnp.bfloat16),
        compiler_params=pltpu.CompilerParams(vmem_limit_bytes=VMEM),
        cost_estimate=pl.CostEstimate(
            flops=16 * SLAB * samples * cores,
            bytes_accessed=2 * SLAB * samples * cores,
            transcendentals=0,
        ),
        name="counts",
    )(ids)


def pool_kernel(counts_ref, arrived_ref, out_ref, total_ref):
    step = pl.program_id(0)
    blocks, cores, depth, width = arrived_ref.shape

    @pl.when(step == 0)
    def _():
        total_ref[...] = jnp.zeros_like(total_ref)

    for core in range(cores):
        total_ref[...] += jnp.dot(
            counts_ref[core],
            arrived_ref[:, core].reshape(blocks * depth, width),
            preferred_element_type=jnp.float32,
        )

    @pl.when(step == pl.num_programs(0) - 1)
    def _():
        out_ref[...] = total_ref[...].astype(out_ref.dtype)


def pool(counts, arrived):
    blocks, cores, depth, width = arrived.shape
    at_once = 8
    return pl.pallas_call(
        pool_kernel,
        grid=(blocks // at_once,),
        in_specs=[
            pl.BlockSpec((cores, SLAB, at_once * depth), lambda i: (0, 0, i)),
            pl.BlockSpec((at_once, cores, depth, width), lambda i: (i, 0, 0, 0)),
        ],
        out_specs=pl.BlockSpec((SLAB, width), lambda i: (0, 0)),
        out_shape=jax.ShapeDtypeStruct((SLAB, width), jnp.bfloat16),
        scratch_shapes=[pltpu.VMEM((SLAB, width), jnp.float32)],
        compiler_params=pltpu.CompilerParams(vmem_limit_bytes=VMEM - 8 * 1024 * 1024),
        cost_estimate=pl.CostEstimate(
            flops=2 * SLAB * blocks * cores * depth * width,
            bytes_accessed=2 * SLAB * blocks * cores * depth,
            transcendentals=0,
        ),
        name="pool",
    )(counts, arrived)


def shards(grads, slots, lengths, rows, accum):
    _, mine, features, width = grads.shape
    positions, samples = slots.shape[2:]
    share = rows.shape[0]
    half = width // CORES
    outgoing = spread(grads.reshape(mine, features, width))
    arrived = lax.all_to_all(
        outgoing.reshape(features * CORES, mine, half), ("shard", "core"), 0, 0, tiled=True
    )
    place = lax.broadcasted_iota(jnp.int32, (positions, samples), 0)
    ids = jnp.where(place < lengths.reshape(1, samples), slots.reshape(positions, samples), -1)
    counts = count_matrix(lax.all_gather(ids, "core", axis=0, tiled=False))
    partial = pool(counts, arrived.reshape(features, CORES, mine, half))
    parts = lax.all_to_all(
        partial.reshape(SLAB // share, share, half), ("chip", "core"), 0, 0, tiled=True
    )
    halves = jnp.sum(
        parts.reshape(SLAB // share // CORES, CORES, share, half).astype(jnp.float32), axis=0
    )
    row_grad = jnp.concatenate([halves[core] for core in range(CORES)], axis=1)
    new_accum = accum + jnp.mean(row_grad * row_grad, axis=1)
    new_rows = rows - STEP_RATE * row_grad / (jnp.sqrt(new_accum)[:, None] + EPSILON)
    serving = lax.all_gather(
        new_rows.astype(jnp.bfloat16), ("chip", "core"), axis=0, tiled=True
    )
    return new_rows, new_accum, serving


def solution(mesh):
    shard, replica = mesh.devices.shape
    split = Mesh(
        mesh.devices.reshape(shard, replica // CORES, CORES), ("shard", "chip", "core")
    )
    replicas = ("chip", "core")
    owners = ("shard", "chip", "core")
    return jax.shard_map(
        shards,
        mesh=split,
        in_specs=(
            P(replicas, "shard", None, None),
            P(replicas, "shard", None, None),
            P(replicas, "shard", None),
            P(owners, None),
            P(owners),
        ),
        out_specs=(P(owners, None), P(owners), P("shard", None)),
        check_vma=False,
    )
```

```python
import jax
import jax.numpy as jnp
from jax import lax
from jax.experimental import pallas as pl
from jax.experimental.pallas import tpu as pltpu
from jax.sharding import Mesh, PartitionSpec as P

SLAB = 1024
STEP_RATE = 0.5
EPSILON = 1e-08
CORES = 2
COUNT = jnp.float8_e4m3fn
VMEM = 56 * 1024 * 1024


def spread_kernel(grads_hbm, out_hbm, grads_ref, out_ref, in_sems, out_sems):
    samples, features, width = grads_ref.shape
    half = width // CORES
    side = features // in_sems.shape[0]
    reads, writes = [], []
    for i, first in enumerate(range(0, features, side)):
        mine = pl.ds(first, side)
        reads.append(
            pltpu.make_async_copy(grads_hbm.at[:, mine], grads_ref.at[:, mine], in_sems.at[i])
        )
        writes.append(pltpu.make_async_copy(out_ref.at[mine], out_hbm.at[mine], out_sems.at[i]))
    for read in reads:
        read.start()
    out_at = lax.broadcasted_iota(jnp.int32, (side * side, side * side), 0)
    in_at = lax.broadcasted_iota(jnp.int32, (side * side, side * side), 1)
    moved = (out_at % side) * side + out_at // side
    permutation = jnp.where(in_at == moved, 1.0, 0.0).astype(jnp.bfloat16)
    for i, first in enumerate(range(0, features, side)):
        reads[i].wait()
        for low in range(0, samples, side):
            block = grads_ref[low : low + side, first : first + side, :]
            turned = jnp.dot(
                permutation,
                block.reshape(side * side, width),
                preferred_element_type=jnp.float32,
            )
            turned = turned.astype(out_ref.dtype).reshape(side, side, width)
            for core in range(CORES):
                out_ref[first : first + side, core, low : low + side] = turned[
                    :, :, core * half : (core + 1) * half
                ]
        writes[i].start()
    for write in writes:
        write.wait()


def spread(grads):
    samples, features, width = grads.shape
    pieces = features // 16
    out = (features, CORES, samples, width // CORES)
    return pl.pallas_call(
        spread_kernel,
        in_specs=[pl.BlockSpec(memory_space=pl.ANY)],
        out_specs=pl.BlockSpec(memory_space=pl.ANY),
        out_shape=jax.ShapeDtypeStruct(out, grads.dtype),
        scratch_shapes=[
            pltpu.VMEM(grads.shape, grads.dtype),
            pltpu.VMEM(out, grads.dtype),
            pltpu.SemaphoreType.DMA((pieces,)),
            pltpu.SemaphoreType.DMA((pieces,)),
        ],
        compiler_params=pltpu.CompilerParams(vmem_limit_bytes=VMEM),
        name="spread",
    )(grads)


def count_kernel(ids_ref, counts_ref):
    positions = ids_ref.shape[1]
    blocks, _, depth, slab = counts_ref.shape
    tall, lanes = 32, 128
    ids = ids_ref[0].T
    lane = lax.broadcasted_iota(jnp.int32, (tall, lanes), 1).astype(jnp.int16)
    one = jnp.ones((tall, lanes), jnp.bfloat16)
    zero = jnp.zeros((tall, lanes), jnp.bfloat16)
    for block in range(blocks):
        for low in range(0, depth, tall):
            first = block * depth + low
            mine = [
                jnp.broadcast_to(ids[first : first + tall, p : p + 1], (tall, lanes)).astype(
                    jnp.int16
                )
                for p in range(positions)
            ]
            for left in range(0, slab, lanes):
                here = lane + jnp.int16(left)
                total = zero
                for p in range(positions):
                    total = total + jnp.where(mine[p] == here, one, zero)
                counts_ref[block, 0, low : low + tall, left : left + lanes] = total.astype(
                    counts_ref.dtype
                )


def count_matrix(ids, depth):
    cores, positions, samples = ids.shape
    blocks = 4
    return pl.pallas_call(
        count_kernel,
        grid=(cores, samples // (blocks * depth)),
        in_specs=[pl.BlockSpec((1, positions, blocks * depth), lambda c, i: (c, 0, i))],
        out_specs=pl.BlockSpec((blocks, 1, depth, SLAB), lambda c, i: (i, c, 0, 0)),
        out_shape=jax.ShapeDtypeStruct((samples // depth, cores, depth, SLAB), COUNT),
        compiler_params=pltpu.CompilerParams(vmem_limit_bytes=VMEM),
        cost_estimate=pl.CostEstimate(
            flops=16 * SLAB * samples * cores,
            bytes_accessed=SLAB * samples * cores,
            transcendentals=0,
        ),
        name="counts",
    )(ids)


def pool_kernel(counts_hbm, arrived_hbm, out_ref, counts_ref, arrived_ref, total_ref, sems):
    pieces = counts_ref.shape[0]
    depth = counts_ref.shape[1]

    def fetch(i):
        return (
            pltpu.make_async_copy(
                counts_hbm.at[pl.ds(i * depth, depth)], counts_ref.at[i], sems.at[0, i]
            ),
            pltpu.make_async_copy(
                arrived_hbm.at[pl.ds(i * depth, depth)], arrived_ref.at[i], sems.at[1, i]
            ),
        )

    copies = [fetch(i) for i in range(pieces)]
    for pair in copies:
        for copy in pair:
            copy.start()
    for i, pair in enumerate(copies):
        for copy in pair:
            copy.wait()
        product = lax.dot_general(
            arrived_ref[i],
            counts_ref[i].astype(jnp.bfloat16),
            (((0,), (0,)), ((), ())),
            preferred_element_type=jnp.float32,
        )
        if i == 0:
            total_ref[...] = product
        elif i < pieces - 1:
            total_ref[...] += product
        else:
            out_ref[...] = (total_ref[...] + product).T.astype(out_ref.dtype)


def pool(counts, arrived, pieces=8):
    samples, width = arrived.shape
    slab = counts.shape[1]
    depth = samples // pieces
    return pl.pallas_call(
        pool_kernel,
        in_specs=[pl.BlockSpec(memory_space=pl.ANY)] * 2,
        out_specs=pl.BlockSpec(memory_space=pltpu.VMEM),
        out_shape=jax.ShapeDtypeStruct((slab, width), jnp.bfloat16),
        scratch_shapes=[
            pltpu.VMEM((pieces, depth, slab), counts.dtype),
            pltpu.VMEM((pieces, depth, width), arrived.dtype),
            pltpu.VMEM((width, slab), jnp.float32),
            pltpu.SemaphoreType.DMA((2, pieces)),
        ],
        compiler_params=pltpu.CompilerParams(vmem_limit_bytes=VMEM - 8 * 1024 * 1024),
        cost_estimate=pl.CostEstimate(
            flops=2 * slab * samples * width,
            bytes_accessed=slab * samples,
            transcendentals=0,
        ),
        name="pool",
    )(counts, arrived)


def shards(grads, slots, lengths, rows, accum):
    _, mine, features, width = grads.shape
    positions, samples = slots.shape[2:]
    share = rows.shape[0]
    half = width // CORES
    outgoing = spread(grads.reshape(mine, features, width))
    arrived = lax.all_to_all(
        outgoing.reshape(features * CORES, mine, half), ("shard", "core"), 0, 0, tiled=True
    )
    place = lax.broadcasted_iota(jnp.int32, (positions, samples), 0)
    ids = jnp.where(place < lengths.reshape(1, samples), slots.reshape(positions, samples), -1)
    counts = count_matrix(lax.all_gather(ids, "core", axis=0, tiled=False), mine)
    partial = pool(
        counts.reshape(CORES * samples, SLAB), arrived.reshape(CORES * samples, half)
    )
    parts = lax.all_to_all(
        partial.reshape(SLAB // share, share, half), ("chip", "core"), 0, 0, tiled=True
    )
    halves = jnp.sum(
        parts.reshape(SLAB // share // CORES, CORES, share, half).astype(jnp.float32), axis=0
    )
    row_grad = jnp.concatenate([halves[core] for core in range(CORES)], axis=1)
    new_accum = accum + jnp.mean(row_grad * row_grad, axis=1)
    new_rows = rows - STEP_RATE * row_grad / (jnp.sqrt(new_accum)[:, None] + EPSILON)
    serving = lax.all_gather(
        new_rows.astype(jnp.bfloat16), ("chip", "core"), axis=0, tiled=True
    )
    return new_rows, new_accum, serving


def solution(mesh):
    shard, replica = mesh.devices.shape
    split = Mesh(
        mesh.devices.reshape(shard, replica // CORES, CORES), ("shard", "chip", "core")
    )
    replicas = ("chip", "core")
    owners = ("shard", "chip", "core")
    return jax.shard_map(
        shards,
        mesh=split,
        in_specs=(
            P(replicas, "shard", None, None),
            P(replicas, "shard", None, None),
            P(replicas, "shard", None),
            P(owners, None),
            P(owners),
        ),
        out_specs=(P(owners, None), P(owners), P("shard", None)),
        check_vma=False,
    )
```

```python
import jax
import jax.numpy as jnp
from jax import lax
from jax.experimental import pallas as pl
from jax.experimental.pallas import tpu as pltpu
from jax.sharding import Mesh, PartitionSpec as P

SLAB = 1024
STEP_RATE = 0.5
EPSILON = 1e-08
CORES = 2
COUNT = jnp.float8_e4m3fn
VMEM = 56 * 1024 * 1024


def spread_kernel(grads_hbm, out_hbm, grads_ref, out_ref, in_sems, out_sems):
    samples, features, width = grads_ref.shape
    half = width // CORES
    side = features // in_sems.shape[0]
    reads, writes = [], []
    for i, first in enumerate(range(0, features, side)):
        mine = pl.ds(first, side)
        reads.append(
            pltpu.make_async_copy(grads_hbm.at[:, mine], grads_ref.at[:, mine], in_sems.at[i])
        )
        writes.append(pltpu.make_async_copy(out_ref.at[mine], out_hbm.at[mine], out_sems.at[i]))
    for read in reads:
        read.start()
    out_at = lax.broadcasted_iota(jnp.int32, (side * side, side * side), 0)
    in_at = lax.broadcasted_iota(jnp.int32, (side * side, side * side), 1)
    moved = (out_at % side) * side + out_at // side
    permutation = jnp.where(in_at == moved, 1.0, 0.0).astype(jnp.bfloat16)
    for i, first in enumerate(range(0, features, side)):
        reads[i].wait()
        for low in range(0, samples, side):
            block = grads_ref[low : low + side, first : first + side, :]
            turned = jnp.dot(
                permutation,
                block.reshape(side * side, width),
                preferred_element_type=jnp.float32,
            )
            turned = turned.astype(out_ref.dtype).reshape(side, side, width)
            for core in range(CORES):
                out_ref[first : first + side, core, low : low + side] = turned[
                    :, :, core * half : (core + 1) * half
                ]
        writes[i].start()
    for write in writes:
        write.wait()


def spread(grads):
    samples, features, width = grads.shape
    pieces = features // 16
    out = (features, CORES, samples, width // CORES)
    return pl.pallas_call(
        spread_kernel,
        in_specs=[pl.BlockSpec(memory_space=pl.ANY)],
        out_specs=pl.BlockSpec(memory_space=pl.ANY),
        out_shape=jax.ShapeDtypeStruct(out, grads.dtype),
        scratch_shapes=[
            pltpu.VMEM(grads.shape, grads.dtype),
            pltpu.VMEM(out, grads.dtype),
            pltpu.SemaphoreType.DMA((pieces,)),
            pltpu.SemaphoreType.DMA((pieces,)),
        ],
        compiler_params=pltpu.CompilerParams(vmem_limit_bytes=VMEM),
        name="spread",
    )(grads)


def count_kernel(ids_ref, counts_ref):
    positions = ids_ref.shape[1]
    blocks, _, depth, slab = counts_ref.shape
    tall, lanes = 32, 128
    ids = ids_ref[0].T
    lane = lax.broadcasted_iota(jnp.int32, (tall, lanes), 1).astype(jnp.int16)
    one = jnp.ones((tall, lanes), jnp.bfloat16)
    zero = jnp.zeros((tall, lanes), jnp.bfloat16)
    for block in range(blocks):
        for low in range(0, depth, tall):
            first = block * depth + low
            mine = [
                jnp.broadcast_to(ids[first : first + tall, p : p + 1], (tall, lanes)).astype(
                    jnp.int16
                )
                for p in range(positions)
            ]
            for left in range(0, slab, lanes):
                here = lane + jnp.int16(left)
                total = zero
                for p in range(positions):
                    total = total + jnp.where(mine[p] == here, one, zero)
                counts_ref[block, 0, low : low + tall, left : left + lanes] = total.astype(
                    counts_ref.dtype
                )


def count_matrix(ids, depth):
    cores, positions, samples = ids.shape
    blocks = 4
    return pl.pallas_call(
        count_kernel,
        grid=(cores, samples // (blocks * depth)),
        in_specs=[pl.BlockSpec((1, positions, blocks * depth), lambda c, i: (c, 0, i))],
        out_specs=pl.BlockSpec((blocks, 1, depth, SLAB), lambda c, i: (i, c, 0, 0)),
        out_shape=jax.ShapeDtypeStruct((samples // depth, cores, depth, SLAB), COUNT),
        compiler_params=pltpu.CompilerParams(vmem_limit_bytes=VMEM),
        cost_estimate=pl.CostEstimate(
            flops=16 * SLAB * samples * cores,
            bytes_accessed=SLAB * samples * cores,
            transcendentals=0,
        ),
        name="counts",
    )(ids)


def pool_kernel(counts_hbm, arrived_hbm, out_ref, counts_ref, arrived_ref, total_ref, sems):
    pieces = counts_ref.shape[0]
    depth = counts_ref.shape[1]

    def fetch(i):
        return (
            pltpu.make_async_copy(
                counts_hbm.at[pl.ds(i * depth, depth)], counts_ref.at[i], sems.at[0, i]
            ),
            pltpu.make_async_copy(
                arrived_hbm.at[pl.ds(i * depth, depth)], arrived_ref.at[i], sems.at[1, i]
            ),
        )

    copies = [fetch(i) for i in range(pieces)]
    for pair in copies:
        for copy in pair:
            copy.start()
    for i, pair in enumerate(copies):
        for copy in pair:
            copy.wait()
        product = lax.dot_general(
            arrived_ref[i],
            counts_ref[i].astype(jnp.bfloat16),
            (((0,), (0,)), ((), ())),
            preferred_element_type=jnp.float32,
        )
        if i == 0:
            total_ref[...] = product
        elif i < pieces - 1:
            total_ref[...] += product
        else:
            pooled = (total_ref[...] + product).T.astype(out_ref.dtype)
            cores, chips, share, _ = out_ref.shape
            for core in range(cores):
                for chip in range(chips):
                    first = (chip * cores + core) * share
                    out_ref[core, chip] = pooled[first : first + share]


def pool(counts, arrived, share, pieces=8):
    samples, width = arrived.shape
    slab = counts.shape[1]
    depth = samples // pieces
    return pl.pallas_call(
        pool_kernel,
        in_specs=[pl.BlockSpec(memory_space=pl.ANY)] * 2,
        out_specs=pl.BlockSpec(memory_space=pltpu.VMEM),
        out_shape=jax.ShapeDtypeStruct(
            (CORES, slab // share // CORES, share, width), jnp.bfloat16
        ),
        scratch_shapes=[
            pltpu.VMEM((pieces, depth, slab), counts.dtype),
            pltpu.VMEM((pieces, depth, width), arrived.dtype),
            pltpu.VMEM((width, slab), jnp.float32),
            pltpu.SemaphoreType.DMA((2, pieces)),
        ],
        compiler_params=pltpu.CompilerParams(vmem_limit_bytes=VMEM - 8 * 1024 * 1024),
        cost_estimate=pl.CostEstimate(
            flops=2 * slab * samples * width,
            bytes_accessed=slab * samples,
            transcendentals=0,
        ),
        name="pool",
    )(counts, arrived)


def update_kernel(parts_ref, rows_ref, accum_ref, new_rows_ref, new_accum_ref, serving_ref):
    cores, chips, _, half = parts_ref.shape
    halves = []
    for core in range(cores):
        total = parts_ref[core, 0].astype(jnp.float32)
        for chip in range(1, chips):
            total = total + parts_ref[core, chip].astype(jnp.float32)
        halves.append(total)
    square = halves[0] * halves[0]
    for total in halves[1:]:
        square = square + total * total
    mean = jnp.sum(square, axis=1, keepdims=True) / (cores * half)
    accum = accum_ref[...].T + mean
    new_accum_ref[...] = accum.T
    scale = STEP_RATE / (jnp.sqrt(accum) + EPSILON)
    for core, total in enumerate(halves):
        mine = slice(core * half, (core + 1) * half)
        fresh = rows_ref[:, mine] - total * scale
        new_rows_ref[:, mine] = fresh
        serving_ref[:, mine] = fresh.astype(serving_ref.dtype)


def update(parts, rows, accum):
    share = rows.shape[0]
    new_rows, new_accum, serving = pl.pallas_call(
        update_kernel,
        out_shape=(
            jax.ShapeDtypeStruct(rows.shape, rows.dtype),
            jax.ShapeDtypeStruct((1, share), accum.dtype),
            jax.ShapeDtypeStruct(rows.shape, jnp.bfloat16),
        ),
        compiler_params=pltpu.CompilerParams(vmem_limit_bytes=8 * 1024 * 1024),
        name="update",
    )(parts, rows, accum.reshape(1, share))
    return new_rows, new_accum.reshape(share), serving


def shards(grads, slots, lengths, rows, accum):
    _, mine, features, width = grads.shape
    positions, samples = slots.shape[2:]
    share = rows.shape[0]
    half = width // CORES
    outgoing = spread(grads.reshape(mine, features, width))
    arrived = lax.all_to_all(
        outgoing.reshape(features * CORES, mine, half), ("shard", "core"), 0, 0, tiled=True
    )
    place = lax.broadcasted_iota(jnp.int32, (positions, samples), 0)
    ids = jnp.where(place < lengths.reshape(1, samples), slots.reshape(positions, samples), -1)
    counts = count_matrix(lax.all_gather(ids, "core", axis=0, tiled=False), mine)
    partial = pool(
        counts.reshape(CORES * samples, SLAB), arrived.reshape(CORES * samples, half), share
    )
    parts = lax.all_to_all(
        partial.reshape(SLAB // share, share, half), ("core", "chip"), 0, 0, tiled=True
    )
    new_rows, new_accum, fresh = update(
        parts.reshape(CORES, SLAB // share // CORES, share, half), rows, accum
    )
    serving = lax.all_gather(fresh, ("chip", "core"), axis=0, tiled=True)
    return new_rows, new_accum, serving


def solution(mesh):
    shard, replica = mesh.devices.shape
    split = Mesh(
        mesh.devices.reshape(shard, replica // CORES, CORES), ("shard", "chip", "core")
    )
    replicas = ("chip", "core")
    owners = ("shard", "chip", "core")
    return jax.shard_map(
        shards,
        mesh=split,
        in_specs=(
            P(replicas, "shard", None, None),
            P(replicas, "shard", None, None),
            P(replicas, "shard", None),
            P(owners, None),
            P(owners),
        ),
        out_specs=(P(owners, None), P(owners), P("shard", None)),
        check_vma=False,
    )
```

```python
import jax
import jax.numpy as jnp
from jax import lax
from jax.experimental import pallas as pl
from jax.experimental.pallas import tpu as pltpu
from jax.sharding import Mesh, PartitionSpec as P

SLAB = 1024
STEP_RATE = 0.5
EPSILON = 1e-08
CORES = 2
COUNT = jnp.float8_e4m3fn
VMEM = 56 * 1024 * 1024


def spread_kernel(grads_hbm, out_hbm, grads_ref, out_ref, in_sems, out_sems):
    samples, features, width = grads_ref.shape
    half = width // CORES
    side = features // in_sems.shape[0]
    reads, writes = [], []
    for i, first in enumerate(range(0, features, side)):
        mine = pl.ds(first, side)
        reads.append(
            pltpu.make_async_copy(grads_hbm.at[:, mine], grads_ref.at[:, mine], in_sems.at[i])
        )
        writes.append(pltpu.make_async_copy(out_ref.at[mine], out_hbm.at[mine], out_sems.at[i]))
    for read in reads:
        read.start()
    for i, first in enumerate(range(0, features, side)):
        reads[i].wait()
        for low in range(0, samples, side):
            block = grads_ref[low : low + side, first : first + side, :]
            turned = jnp.swapaxes(block, 0, 1)
            for core in range(CORES):
                out_ref[first : first + side, core, low : low + side] = turned[
                    :, :, core * half : (core + 1) * half
                ]
        writes[i].start()
    for write in writes:
        write.wait()


def spread(grads):
    samples, features, width = grads.shape
    pieces = features // 16
    out = (features, CORES, samples, width // CORES)
    return pl.pallas_call(
        spread_kernel,
        in_specs=[pl.BlockSpec(memory_space=pl.ANY)],
        out_specs=pl.BlockSpec(memory_space=pl.ANY),
        out_shape=jax.ShapeDtypeStruct(out, grads.dtype),
        scratch_shapes=[
            pltpu.VMEM(grads.shape, grads.dtype),
            pltpu.VMEM(out, grads.dtype),
            pltpu.SemaphoreType.DMA((pieces,)),
            pltpu.SemaphoreType.DMA((pieces,)),
        ],
        compiler_params=pltpu.CompilerParams(vmem_limit_bytes=VMEM),
        name="spread",
    )(grads)


def count_kernel(ids_ref, counts_ref):
    positions = ids_ref.shape[1]
    blocks, _, depth, slab = counts_ref.shape
    tall, lanes = 32, 128
    ids = ids_ref[0].T
    lane = lax.broadcasted_iota(jnp.int32, (tall, lanes), 1).astype(jnp.int16)
    one = jnp.ones((tall, lanes), jnp.bfloat16)
    zero = jnp.zeros((tall, lanes), jnp.bfloat16)
    for block in range(blocks):
        for low in range(0, depth, tall):
            first = block * depth + low
            mine = [
                jnp.broadcast_to(ids[first : first + tall, p : p + 1], (tall, lanes)).astype(
                    jnp.int16
                )
                for p in range(positions)
            ]
            for left in range(0, slab, lanes):
                here = lane + jnp.int16(left)
                total = zero
                for p in range(positions):
                    total = total + jnp.where(mine[p] == here, one, zero)
                counts_ref[block, 0, low : low + tall, left : left + lanes] = total.astype(
                    counts_ref.dtype
                )


def count_matrix(ids, depth):
    cores, positions, samples = ids.shape
    blocks = 4
    return pl.pallas_call(
        count_kernel,
        grid=(cores, samples // (blocks * depth)),
        in_specs=[pl.BlockSpec((1, positions, blocks * depth), lambda c, i: (c, 0, i))],
        out_specs=pl.BlockSpec((blocks, 1, depth, SLAB), lambda c, i: (i, c, 0, 0)),
        out_shape=jax.ShapeDtypeStruct((samples // depth, cores, depth, SLAB), COUNT),
        compiler_params=pltpu.CompilerParams(vmem_limit_bytes=VMEM),
        cost_estimate=pl.CostEstimate(
            flops=16 * SLAB * samples * cores,
            bytes_accessed=SLAB * samples * cores,
            transcendentals=0,
        ),
        name="counts",
    )(ids)


def pool_kernel(counts_hbm, arrived_hbm, out_ref, counts_ref, arrived_ref, total_ref, sems):
    pieces = counts_ref.shape[0]
    depth = counts_ref.shape[1]

    def fetch(i):
        return (
            pltpu.make_async_copy(
                counts_hbm.at[pl.ds(i * depth, depth)], counts_ref.at[i], sems.at[0, i]
            ),
            pltpu.make_async_copy(
                arrived_hbm.at[pl.ds(i * depth, depth)], arrived_ref.at[i], sems.at[1, i]
            ),
        )

    copies = [fetch(i) for i in range(pieces)]
    for pair in copies:
        for copy in pair:
            copy.start()
    for i, pair in enumerate(copies):
        for copy in pair:
            copy.wait()
        product = lax.dot_general(
            arrived_ref[i],
            counts_ref[i].astype(jnp.bfloat16),
            (((0,), (0,)), ((), ())),
            preferred_element_type=jnp.float32,
        )
        if i == 0:
            total_ref[...] = product
        elif i < pieces - 1:
            total_ref[...] += product
        else:
            pooled = (total_ref[...] + product).T.astype(out_ref.dtype)
            cores, chips, share, _ = out_ref.shape
            for core in range(cores):
                for chip in range(chips):
                    first = (chip * cores + core) * share
                    out_ref[core, chip] = pooled[first : first + share]


def pool(counts, arrived, share, pieces=8):
    samples, width = arrived.shape
    slab = counts.shape[1]
    depth = samples // pieces
    return pl.pallas_call(
        pool_kernel,
        in_specs=[pl.BlockSpec(memory_space=pl.ANY)] * 2,
        out_specs=pl.BlockSpec(memory_space=pltpu.VMEM),
        out_shape=jax.ShapeDtypeStruct(
            (CORES, slab // share // CORES, share, width), jnp.bfloat16
        ),
        scratch_shapes=[
            pltpu.VMEM((pieces, depth, slab), counts.dtype),
            pltpu.VMEM((pieces, depth, width), arrived.dtype),
            pltpu.VMEM((width, slab), jnp.float32),
            pltpu.SemaphoreType.DMA((2, pieces)),
        ],
        compiler_params=pltpu.CompilerParams(vmem_limit_bytes=VMEM - 8 * 1024 * 1024),
        cost_estimate=pl.CostEstimate(
            flops=2 * slab * samples * width,
            bytes_accessed=slab * samples,
            transcendentals=0,
        ),
        name="pool",
    )(counts, arrived)


def update_kernel(parts_ref, rows_ref, accum_ref, new_rows_ref, new_accum_ref, serving_ref):
    cores, chips, _, half = parts_ref.shape
    halves = []
    for core in range(cores):
        total = parts_ref[core, 0].astype(jnp.float32)
        for chip in range(1, chips):
            total = total + parts_ref[core, chip].astype(jnp.float32)
        halves.append(total)
    square = halves[0] * halves[0]
    for total in halves[1:]:
        square = square + total * total
    mean = jnp.sum(square, axis=1, keepdims=True) / (cores * half)
    accum = accum_ref[...].T + mean
    new_accum_ref[...] = accum.T
    scale = STEP_RATE / (jnp.sqrt(accum) + EPSILON)
    for core, total in enumerate(halves):
        mine = slice(core * half, (core + 1) * half)
        fresh = rows_ref[:, mine] - total * scale
        new_rows_ref[:, mine] = fresh
        for chip in range(chips):
            serving_ref[chip, :, mine] = fresh.astype(serving_ref.dtype)


def update(parts, rows, accum):
    share = rows.shape[0]
    new_rows, new_accum, serving = pl.pallas_call(
        update_kernel,
        out_shape=(
            jax.ShapeDtypeStruct(rows.shape, rows.dtype),
            jax.ShapeDtypeStruct((1, share), accum.dtype),
            jax.ShapeDtypeStruct((parts.shape[1],) + rows.shape, jnp.bfloat16),
        ),
        compiler_params=pltpu.CompilerParams(vmem_limit_bytes=8 * 1024 * 1024),
        name="update",
    )(parts, rows, accum.reshape(1, share))
    return new_rows, new_accum.reshape(share), serving


def shards(grads, slots, lengths, rows, accum):
    _, mine, features, width = grads.shape
    positions, samples = slots.shape[2:]
    share = rows.shape[0]
    half = width // CORES
    outgoing = spread(grads.reshape(mine, features, width))
    arrived = lax.all_to_all(
        outgoing.reshape(features * CORES, mine, half), ("shard", "core"), 0, 0, tiled=True
    )
    place = lax.broadcasted_iota(jnp.int32, (positions, samples), 0)
    ids = jnp.where(place < lengths.reshape(1, samples), slots.reshape(positions, samples), -1)
    counts = count_matrix(lax.all_gather(ids, "core", axis=0, tiled=False), mine)
    partial = pool(
        counts.reshape(CORES * samples, SLAB), arrived.reshape(CORES * samples, half), share
    )
    parts = lax.all_to_all(
        partial.reshape(SLAB // share, share, half), ("core", "chip"), 0, 0, tiled=True
    )
    new_rows, new_accum, fresh = update(
        parts.reshape(CORES, SLAB // share // CORES, share, half), rows, accum
    )
    alike = lax.all_to_all(fresh, "chip", 0, 0, tiled=True)
    pairs = lax.all_gather(alike, "core", axis=0, tiled=False)
    serving = pairs.transpose(1, 0, 2, 3).reshape(SLAB, width)
    return new_rows, new_accum, serving


def solution(mesh):
    shard, replica = mesh.devices.shape
    split = Mesh(
        mesh.devices.reshape(shard, replica // CORES, CORES), ("shard", "chip", "core")
    )
    replicas = ("chip", "core")
    owners = ("shard", "chip", "core")
    return jax.shard_map(
        shards,
        mesh=split,
        in_specs=(
            P(replicas, "shard", None, None),
            P(replicas, "shard", None, None),
            P(replicas, "shard", None),
            P(owners, None),
            P(owners),
        ),
        out_specs=(P(owners, None), P(owners), P("shard", None)),
        check_vma=False,
    )
```

```python
import jax
import jax.numpy as jnp
from jax import lax
from jax.experimental import pallas as pl
from jax.experimental.pallas import tpu as pltpu
from jax.sharding import Mesh, PartitionSpec as P

SLAB = 1024
STEP_RATE = 0.5
EPSILON = 1e-08
CORES = 2
COUNT = jnp.int4
VMEM = 56 * 1024 * 1024


def spread_kernel(grads_hbm, out_hbm, grads_ref, out_ref, in_sems, out_sems):
    samples, features, width = grads_ref.shape
    half = width // CORES
    side = features // in_sems.shape[0]
    reads, writes = [], []
    for i, first in enumerate(range(0, features, side)):
        mine = pl.ds(first, side)
        reads.append(
            pltpu.make_async_copy(grads_hbm.at[:, mine], grads_ref.at[:, mine], in_sems.at[i])
        )
        writes.append(pltpu.make_async_copy(out_ref.at[mine], out_hbm.at[mine], out_sems.at[i]))
    for read in reads:
        read.start()
    for i, first in enumerate(range(0, features, side)):
        reads[i].wait()
        for low in range(0, samples, side):
            block = grads_ref[low : low + side, first : first + side, :]
            turned = jnp.swapaxes(block, 0, 1)
            for core in range(CORES):
                out_ref[first : first + side, core, low : low + side] = turned[
                    :, :, core * half : (core + 1) * half
                ]
        writes[i].start()
    for write in writes:
        write.wait()


def spread(grads):
    samples, features, width = grads.shape
    pieces = features // 16
    out = (features, CORES, samples, width // CORES)
    return pl.pallas_call(
        spread_kernel,
        in_specs=[pl.BlockSpec(memory_space=pl.ANY)],
        out_specs=pl.BlockSpec(memory_space=pl.ANY),
        out_shape=jax.ShapeDtypeStruct(out, grads.dtype),
        scratch_shapes=[
            pltpu.VMEM(grads.shape, grads.dtype),
            pltpu.VMEM(out, grads.dtype),
            pltpu.SemaphoreType.DMA((pieces,)),
            pltpu.SemaphoreType.DMA((pieces,)),
        ],
        compiler_params=pltpu.CompilerParams(vmem_limit_bytes=VMEM),
        name="spread",
    )(grads)


def count_kernel(ids_ref, counts_ref):
    positions = ids_ref.shape[1]
    blocks, _, depth, slab = counts_ref.shape
    tall, lanes = 64, 128
    ids = ids_ref[0].T
    lane = lax.broadcasted_iota(jnp.int32, (tall, lanes), 1).astype(jnp.int16)
    one = jnp.full((tall, lanes), -1, jnp.int16)
    zero = jnp.zeros((tall, lanes), jnp.int16)
    for block in range(blocks):
        for low in range(0, depth, tall):
            first = block * depth + low
            mine = [
                jnp.broadcast_to(ids[first : first + tall, p : p + 1], (tall, lanes)).astype(
                    jnp.int16
                )
                for p in range(positions)
            ]
            for left in range(0, slab, lanes):
                here = lane + jnp.int16(left)
                total = zero
                for p in range(positions):
                    total = total + jnp.where(mine[p] == here, one, zero)
                counts_ref[block, 0, low : low + tall, left : left + lanes] = total.astype(
                    counts_ref.dtype
                )


def count_matrix(ids, depth):
    cores, positions, samples = ids.shape
    blocks = 4
    return pl.pallas_call(
        count_kernel,
        grid=(cores, samples // (blocks * depth)),
        in_specs=[pl.BlockSpec((1, positions, blocks * depth), lambda c, i: (c, 0, i))],
        out_specs=pl.BlockSpec((blocks, 1, depth, SLAB), lambda c, i: (i, c, 0, 0)),
        out_shape=jax.ShapeDtypeStruct((samples // depth, cores, depth, SLAB), COUNT),
        compiler_params=pltpu.CompilerParams(vmem_limit_bytes=VMEM),
        cost_estimate=pl.CostEstimate(
            flops=16 * SLAB * samples * cores,
            bytes_accessed=SLAB * samples * cores,
            transcendentals=0,
        ),
        name="counts",
    )(ids)


def pool_kernel(counts_hbm, arrived_hbm, out_ref, counts_ref, arrived_ref, total_ref, sems):
    pieces = counts_ref.shape[0]
    depth = counts_ref.shape[1]

    def fetch(i):
        return (
            pltpu.make_async_copy(
                counts_hbm.at[pl.ds(i * depth, depth)], counts_ref.at[i], sems.at[0, i]
            ),
            pltpu.make_async_copy(
                arrived_hbm.at[pl.ds(i * depth, depth)], arrived_ref.at[i], sems.at[1, i]
            ),
        )

    copies = [fetch(i) for i in range(pieces)]
    for pair in copies:
        for copy in pair:
            copy.start()
    for i, pair in enumerate(copies):
        for copy in pair:
            copy.wait()
        product = lax.dot_general(
            arrived_ref[i],
            counts_ref[i].astype(jnp.bfloat16),
            (((0,), (0,)), ((), ())),
            preferred_element_type=jnp.float32,
        )
        if i == 0:
            total_ref[...] = product
        elif i < pieces - 1:
            total_ref[...] += product
        else:
            pooled = (-total_ref[...] - product).T.astype(out_ref.dtype)
            cores, chips, share, _ = out_ref.shape
            for core in range(cores):
                for chip in range(chips):
                    first = (chip * cores + core) * share
                    out_ref[core, chip] = pooled[first : first + share]


def pool(counts, arrived, share, pieces=4):
    samples, width = arrived.shape
    slab = counts.shape[1]
    depth = samples // pieces
    return pl.pallas_call(
        pool_kernel,
        in_specs=[pl.BlockSpec(memory_space=pl.ANY)] * 2,
        out_specs=pl.BlockSpec(memory_space=pltpu.VMEM),
        out_shape=jax.ShapeDtypeStruct(
            (CORES, slab // share // CORES, share, width), jnp.bfloat16
        ),
        scratch_shapes=[
            pltpu.VMEM((pieces, depth, slab), counts.dtype),
            pltpu.VMEM((pieces, depth, width), arrived.dtype),
            pltpu.VMEM((width, slab), jnp.float32),
            pltpu.SemaphoreType.DMA((2, pieces)),
        ],
        compiler_params=pltpu.CompilerParams(vmem_limit_bytes=VMEM - 8 * 1024 * 1024),
        cost_estimate=pl.CostEstimate(
            flops=2 * slab * samples * width,
            bytes_accessed=slab * samples,
            transcendentals=0,
        ),
        name="pool",
    )(counts, arrived)


def update_kernel(parts_ref, rows_ref, accum_ref, new_rows_ref, new_accum_ref, serving_ref):
    cores, chips, _, half = parts_ref.shape
    halves = []
    for core in range(cores):
        total = parts_ref[core, 0].astype(jnp.float32)
        for chip in range(1, chips):
            total = total + parts_ref[core, chip].astype(jnp.float32)
        halves.append(total)
    square = halves[0] * halves[0]
    for total in halves[1:]:
        square = square + total * total
    mean = jnp.sum(square, axis=1, keepdims=True) / (cores * half)
    accum = accum_ref[...].T + mean
    new_accum_ref[...] = accum.T
    scale = STEP_RATE / (jnp.sqrt(accum) + EPSILON)
    for core, total in enumerate(halves):
        mine = slice(core * half, (core + 1) * half)
        fresh = rows_ref[:, mine] - total * scale
        new_rows_ref[:, mine] = fresh
        for chip in range(chips):
            serving_ref[chip, :, mine] = fresh.astype(serving_ref.dtype)


def update(parts, rows, accum):
    share = rows.shape[0]
    new_rows, new_accum, serving = pl.pallas_call(
        update_kernel,
        out_shape=(
            jax.ShapeDtypeStruct(rows.shape, rows.dtype),
            jax.ShapeDtypeStruct((1, share), accum.dtype),
            jax.ShapeDtypeStruct((parts.shape[1],) + rows.shape, jnp.bfloat16),
        ),
        compiler_params=pltpu.CompilerParams(vmem_limit_bytes=8 * 1024 * 1024),
        name="update",
    )(parts, rows, accum.reshape(1, share))
    return new_rows, new_accum.reshape(share), serving


def shards(grads, slots, lengths, rows, accum):
    _, mine, features, width = grads.shape
    positions, samples = slots.shape[2:]
    share = rows.shape[0]
    half = width // CORES
    outgoing = spread(grads.reshape(mine, features, width))
    arrived = lax.all_to_all(
        outgoing.reshape(features * CORES, mine, half), ("shard", "core"), 0, 0, tiled=True
    )
    place = lax.broadcasted_iota(jnp.int32, (positions, samples), 0)
    ids = jnp.where(place < lengths.reshape(1, samples), slots.reshape(positions, samples), -1)
    counts = count_matrix(lax.all_gather(ids, "core", axis=0, tiled=False), mine)
    partial = pool(
        counts.reshape(CORES * samples, SLAB), arrived.reshape(CORES * samples, half), share
    )
    parts = lax.all_to_all(
        partial.reshape(SLAB // share, share, half), ("core", "chip"), 0, 0, tiled=True
    )
    new_rows, new_accum, fresh = update(
        parts.reshape(CORES, SLAB // share // CORES, share, half), rows, accum
    )
    alike = lax.all_to_all(fresh, "chip", 0, 0, tiled=True)
    pairs = lax.all_gather(alike, "core", axis=0, tiled=False)
    serving = pairs.transpose(1, 0, 2, 3).reshape(SLAB, width)
    return new_rows, new_accum, serving


def solution(mesh):
    shard, replica = mesh.devices.shape
    split = Mesh(
        mesh.devices.reshape(shard, replica // CORES, CORES), ("shard", "chip", "core")
    )
    replicas = ("chip", "core")
    owners = ("shard", "chip", "core")
    return jax.shard_map(
        shards,
        mesh=split,
        in_specs=(
            P(replicas, "shard", None, None),
            P(replicas, "shard", None, None),
            P(replicas, "shard", None),
            P(owners, None),
            P(owners),
        ),
        out_specs=(P(owners, None), P(owners), P("shard", None)),
        check_vma=False,
    )
```

```python
import jax
import jax.numpy as jnp
from jax import lax
from jax.experimental import pallas as pl
from jax.experimental.pallas import tpu as pltpu
from jax.sharding import Mesh, PartitionSpec as P

SLAB = 1024
STEP_RATE = 0.5
EPSILON = 1e-08
CORES = 2
CUTS = (0, 1, 4, 8, 12, 16)
COUNT = jnp.int4
VMEM = 56 * 1024 * 1024


def spread_kernel(grads_hbm, out_hbm, grads_ref, out_ref, in_sems, out_sems):
    samples, features, width = grads_ref.shape
    half = width // CORES
    side = features // in_sems.shape[0]
    reads, writes = [], []
    for i, first in enumerate(range(0, features, side)):
        mine = pl.ds(first, side)
        reads.append(
            pltpu.make_async_copy(grads_hbm.at[:, mine], grads_ref.at[:, mine], in_sems.at[i])
        )
        writes.append(pltpu.make_async_copy(out_ref.at[mine], out_hbm.at[mine], out_sems.at[i]))
    for read in reads:
        read.start()
    for i, first in enumerate(range(0, features, side)):
        reads[i].wait()
        for low in range(0, samples, side):
            block = grads_ref[low : low + side, first : first + side, :]
            turned = jnp.swapaxes(block, 0, 1)
            for core in range(CORES):
                out_ref[first : first + side, core, low : low + side] = turned[
                    :, :, core * half : (core + 1) * half
                ]
        writes[i].start()
    for write in writes:
        write.wait()


def spread(grads):
    samples, features, width = grads.shape
    pieces = features // 16
    out = (features, CORES, samples, width // CORES)
    return pl.pallas_call(
        spread_kernel,
        in_specs=[pl.BlockSpec(memory_space=pl.ANY)],
        out_specs=pl.BlockSpec(memory_space=pl.ANY),
        out_shape=jax.ShapeDtypeStruct(out, grads.dtype),
        scratch_shapes=[
            pltpu.VMEM(grads.shape, grads.dtype),
            pltpu.VMEM(out, grads.dtype),
            pltpu.SemaphoreType.DMA((pieces,)),
            pltpu.SemaphoreType.DMA((pieces,)),
        ],
        compiler_params=pltpu.CompilerParams(vmem_limit_bytes=VMEM),
        name="spread",
    )(grads)


def count_kernel(ids_ref, counts_ref):
    positions = ids_ref.shape[1]
    blocks, _, depth, slab = counts_ref.shape
    tall, lanes = 64, 128
    ids = ids_ref[0].T
    lane = lax.broadcasted_iota(jnp.int32, (tall, lanes), 1).astype(jnp.int16)
    one = jnp.full((tall, lanes), -1, jnp.int16)
    zero = jnp.zeros((tall, lanes), jnp.int16)
    for block in range(blocks):
        for low in range(0, depth, tall):
            first = block * depth + low
            mine = [
                jnp.broadcast_to(ids[first : first + tall, p : p + 1], (tall, lanes)).astype(
                    jnp.int16
                )
                for p in range(positions)
            ]
            for left in range(0, slab, lanes):
                here = lane + jnp.int16(left)
                total = zero
                for p in range(positions):
                    total = total + jnp.where(mine[p] == here, one, zero)
                counts_ref[block, 0, low : low + tall, left : left + lanes] = total.astype(
                    counts_ref.dtype
                )


def count_matrix(ids, depth):
    cores, positions, samples = ids.shape
    blocks = 4
    return pl.pallas_call(
        count_kernel,
        grid=(cores, samples // (blocks * depth)),
        in_specs=[pl.BlockSpec((1, positions, blocks * depth), lambda c, i: (c, 0, i))],
        out_specs=pl.BlockSpec((blocks, 1, depth, SLAB), lambda c, i: (i, c, 0, 0)),
        out_shape=jax.ShapeDtypeStruct((samples // depth, cores, depth, SLAB), COUNT),
        compiler_params=pltpu.CompilerParams(vmem_limit_bytes=VMEM),
        cost_estimate=pl.CostEstimate(
            flops=16 * SLAB * samples * cores,
            bytes_accessed=SLAB * samples * cores,
            transcendentals=0,
        ),
        name="counts",
    )(ids)


def pool_kernel(counts_hbm, arrived_hbm, out_ref, counts_ref, arrived_ref, total_ref, sems):
    samples = counts_ref.shape[0]
    edges = [samples * cut // 16 for cut in CUTS]
    pieces = len(CUTS) - 1
    copies = []
    for i in range(pieces):
        mine = pl.ds(edges[i], edges[i + 1] - edges[i])
        copies.append(
            (
                pltpu.make_async_copy(counts_hbm.at[mine], counts_ref.at[mine], sems.at[0, i]),
                pltpu.make_async_copy(arrived_hbm.at[mine], arrived_ref.at[mine], sems.at[1, i]),
            )
        )
    for pair in copies:
        for copy in pair:
            copy.start()
    for i, pair in enumerate(copies):
        for copy in pair:
            copy.wait()
        product = lax.dot_general(
            arrived_ref[edges[i] : edges[i + 1]],
            counts_ref[edges[i] : edges[i + 1]].astype(jnp.bfloat16),
            (((0,), (0,)), ((), ())),
            preferred_element_type=jnp.float32,
        )
        if i == 0:
            total_ref[...] = product
        elif i < pieces - 1:
            total_ref[...] += product
        else:
            pooled = (-total_ref[...] - product).T.astype(out_ref.dtype)
            cores, chips, share, _ = out_ref.shape
            for core in range(cores):
                for chip in range(chips):
                    first = (chip * cores + core) * share
                    out_ref[core, chip] = pooled[first : first + share]


def pool(counts, arrived, share):
    samples, width = arrived.shape
    slab = counts.shape[1]
    return pl.pallas_call(
        pool_kernel,
        in_specs=[pl.BlockSpec(memory_space=pl.ANY)] * 2,
        out_specs=pl.BlockSpec(memory_space=pltpu.VMEM),
        out_shape=jax.ShapeDtypeStruct(
            (CORES, slab // share // CORES, share, width), jnp.bfloat16
        ),
        scratch_shapes=[
            pltpu.VMEM((samples, slab), counts.dtype),
            pltpu.VMEM((samples, width), arrived.dtype),
            pltpu.VMEM((width, slab), jnp.float32),
            pltpu.SemaphoreType.DMA((2, len(CUTS) - 1)),
        ],
        compiler_params=pltpu.CompilerParams(vmem_limit_bytes=VMEM - 8 * 1024 * 1024),
        cost_estimate=pl.CostEstimate(
            flops=2 * slab * samples * width,
            bytes_accessed=slab * samples,
            transcendentals=0,
        ),
        name="pool",
    )(counts, arrived)


def update_kernel(parts_ref, rows_ref, accum_ref, new_rows_ref, new_accum_ref, serving_ref):
    cores, chips, _, half = parts_ref.shape
    halves = []
    for core in range(cores):
        total = parts_ref[core, 0].astype(jnp.float32)
        for chip in range(1, chips):
            total = total + parts_ref[core, chip].astype(jnp.float32)
        halves.append(total)
    square = halves[0] * halves[0]
    for total in halves[1:]:
        square = square + total * total
    mean = jnp.sum(square, axis=1, keepdims=True) / (cores * half)
    accum = accum_ref[...].T + mean
    new_accum_ref[...] = accum.T
    scale = STEP_RATE / (jnp.sqrt(accum) + EPSILON)
    for core, total in enumerate(halves):
        mine = slice(core * half, (core + 1) * half)
        fresh = rows_ref[:, mine] - total * scale
        new_rows_ref[:, mine] = fresh
        for chip in range(chips):
            serving_ref[chip, :, mine] = fresh.astype(serving_ref.dtype)


def update(parts, rows, accum):
    share = rows.shape[0]
    new_rows, new_accum, serving = pl.pallas_call(
        update_kernel,
        out_shape=(
            jax.ShapeDtypeStruct(rows.shape, rows.dtype),
            jax.ShapeDtypeStruct((1, share), accum.dtype),
            jax.ShapeDtypeStruct((parts.shape[1],) + rows.shape, jnp.bfloat16),
        ),
        compiler_params=pltpu.CompilerParams(vmem_limit_bytes=8 * 1024 * 1024),
        name="update",
    )(parts, rows, accum.reshape(1, share))
    return new_rows, new_accum.reshape(share), serving


def shards(grads, slots, lengths, rows, accum):
    _, mine, features, width = grads.shape
    positions, samples = slots.shape[2:]
    share = rows.shape[0]
    half = width // CORES
    outgoing = spread(grads.reshape(mine, features, width))
    arrived = lax.all_to_all(
        outgoing.reshape(features * CORES, mine, half), ("shard", "core"), 0, 0, tiled=True
    )
    place = lax.broadcasted_iota(jnp.int32, (positions, samples), 0)
    ids = jnp.where(place < lengths.reshape(1, samples), slots.reshape(positions, samples), -1)
    counts = count_matrix(lax.all_gather(ids, "core", axis=0, tiled=False), mine)
    partial = pool(
        counts.reshape(CORES * samples, SLAB), arrived.reshape(CORES * samples, half), share
    )
    parts = lax.all_to_all(
        partial.reshape(SLAB // share, share, half), ("core", "chip"), 0, 0, tiled=True
    )
    new_rows, new_accum, fresh = update(
        parts.reshape(CORES, SLAB // share // CORES, share, half), rows, accum
    )
    alike = lax.all_to_all(fresh, "chip", 0, 0, tiled=True)
    pairs = lax.all_gather(alike, "core", axis=0, tiled=False)
    serving = pairs.transpose(1, 0, 2, 3).reshape(SLAB, width)
    return new_rows, new_accum, serving


def solution(mesh):
    shard, replica = mesh.devices.shape
    split = Mesh(
        mesh.devices.reshape(shard, replica // CORES, CORES), ("shard", "chip", "core")
    )
    replicas = ("chip", "core")
    owners = ("shard", "chip", "core")
    return jax.shard_map(
        shards,
        mesh=split,
        in_specs=(
            P(replicas, "shard", None, None),
            P(replicas, "shard", None, None),
            P(replicas, "shard", None),
            P(owners, None),
            P(owners),
        ),
        out_specs=(P(owners, None), P(owners), P("shard", None)),
        check_vma=False,
    )
```
